256 devices in a mesh: inst: 8 (over y, core), rank: 32 (over x, z).
Axes of the slice: x: 4, y: 4, z: 8, core: 2. Of those that a mesh axis runs over, the one named last changes fastest.
Arguments:
- ffn_rows: bfloat16 [4096, 7168], P(('inst', 'rank')), parts along dimension 0, may hold values from -6 to 6
- row_counts: int32 [256], P('inst'), parts along dimension 0, may hold values from 1 to 16, as said below
- gate_weight: bfloat16 [7168, 9216], P(None, 'rank'), may hold values from -0.0625 to 0.0625
- up_weight: bfloat16 [7168, 9216], P(None, 'rank'), may hold values from -0.0625 to 0.0625
- down_weight: bfloat16 [9216, 7168], P('rank'), may hold values from -0.0625 to 0.0625
- queries: bfloat16 [1024, 64, 576], P(('inst', 'rank')), parts along dimension 0, may hold values from -20 to 20
- latent_cache: bfloat16 [1024, 64, 576], P(('inst', 'rank')), parts along dimension 0, may hold values from -6 to 6
- live_requests: int32 [256], P('inst'), parts along dimension 0, may hold values from 1 to 4, as said below
- cache_lengths: int32 [1024], P('inst'), parts along dimension 0, may hold values from 1 to 64, as said below
Outputs:
- ffn_out: bfloat16 [4096, 7168], P(('inst', 'rank')), parts along dimension 0
- attn_latent: bfloat16 [1024, 64, 512], P(('inst', 'rank')), parts along dimension 0
The draws below stay inside these ranges and needn't reach their ends.
There are 8 independent parts, one for each index of `inst`. The reference program is written for one: setup_inputs(seed, part) draws one part's arguments, and reference() takes and returns one part's arrays. A program takes and returns all parts, laid end to end along the dimension named above; an argument that names none is the same for every part. Nothing has to cross between parts.
Inputs may be any that keep to these rules, and one draw needn't show every extreme that they name: `row_counts`: some rank has all its token slots live. `live_requests`: some rank has all its request slots live. `cache_lengths`: some slot is full.
All inputs are finite; a program needn't handle non-finite values.
Results may differ from the reference program's by a relative error of at most 0.011.
Values may be sent and summed in bfloat16 or wider, within the bound.
A program may use at most 128 MiB of HBM per device.

```python
import jax
import jax.numpy as jnp

D = 7168
FF = 9216
HEADS = 64
LATENT = 512
ROPE = 64
SLOTS = 4
CTX = 64
ROWS_DEV = 16
ROWS = 512
N_RANK = 32


def cache_base(key):
    values = jax.random.normal(key, (SLOTS * N_RANK, CTX, LATENT + ROPE), jnp.float32)
    return jnp.clip(values, -6.0, 6.0)


def draw_latent_cache(key, part):
    base = cache_base(key)
    return base.astype(jnp.bfloat16)


def draw_queries(key, part):
    key = jax.random.fold_in(key, 5)
    values = jax.random.normal(key, (SLOTS * N_RANK, HEADS, LATENT + ROPE), jnp.float32)
    return jnp.clip(values, -20.0, 20.0).astype(jnp.bfloat16)


def full_counts(key, total, highest):
    counts = jax.random.randint(key, (total,), 1, highest + 1)
    where_full = jax.random.randint(jax.random.fold_in(key, 1), (), 0, total)
    return counts.at[where_full].set(highest).astype(jnp.int32)


def draw_row_counts(key, part):
    key = jax.random.fold_in(key, 13)
    return full_counts(key, N_RANK, ROWS_DEV)


def draw_live_requests(key, part):
    key = jax.random.fold_in(key, 17)
    return full_counts(key, N_RANK, SLOTS)


def draw_cache_lengths(key, part):
    key = jax.random.fold_in(key, 19)
    return full_counts(key, SLOTS * N_RANK, CTX)


def block_scale(own_key, shape, cuts, low, high):
    level = 1.0
    for axis_at, blocks in cuts:
        draws = jax.random.uniform(jax.random.fold_in(jax.random.fold_in(own_key, 6), axis_at), (blocks,), jnp.float32, low / len(cuts), high / len(cuts))
        level = level * jnp.repeat(jnp.exp(draws), shape[axis_at] // blocks).reshape((-1,) + (1,) * (len(shape) - 1 - axis_at))
    return level


def bell_draw(stream_key, extent, spread, bound, cuts=(), kind=jnp.bfloat16):
    result = spread * jax.random.normal(stream_key, extent, jnp.float32)
    if cuts:
        result = result * block_scale(stream_key, extent, cuts, -0.22, 0.18)
    return jnp.clip(result, -bound, bound).astype(kind)


def setup_inputs(seed: int = 0, part: int = 0) -> dict:
    key_of = jax.random.split(jax.random.key(seed), 10)
    part_keys = jax.random.split(jax.random.fold_in(key_of[9], part), 10)
    ffn_rows = bell_draw(part_keys[0], (ROWS, D), 1.0, 6.0, ((0, 32),))
    row_counts = draw_row_counts(jax.random.fold_in(jax.random.fold_in(key_of[9], part), 71), part)
    gate_weight = bell_draw(key_of[2], (D, FF), D ** -0.5, 0.0625, ((1, 32),))
    up_weight = bell_draw(key_of[3], (D, FF), D ** -0.5, 0.0625, ((1, 32),))
    down_weight = bell_draw(key_of[4], (FF, D), FF ** -0.5, 0.0625, ((0, 32),))
    queries = draw_queries(jax.random.fold_in(jax.random.fold_in(key_of[9], part), 71), part)
    latent_cache = draw_latent_cache(jax.random.fold_in(jax.random.fold_in(key_of[9], part), 71), part)
    live_requests = draw_live_requests(jax.random.fold_in(jax.random.fold_in(key_of[9], part), 71), part)
    cache_lengths = draw_cache_lengths(jax.random.fold_in(jax.random.fold_in(key_of[9], part), 71), part)
    return dict(ffn_rows=ffn_rows, row_counts=row_counts, gate_weight=gate_weight, up_weight=up_weight, down_weight=down_weight, queries=queries, latent_cache=latent_cache, live_requests=live_requests, cache_lengths=cache_lengths)


score_scale = 192.0 ** -0.5


def reference(ffn_rows, row_counts, gate_weight, up_weight, down_weight, queries, latent_cache, live_requests, cache_lengths):
    row_index = jnp.arange(ROWS_DEV * N_RANK)
    row_live = (row_index % ROWS_DEV) < row_counts[row_index // ROWS_DEV]
    rows_in = jnp.where(row_live[:, None], ffn_rows, jnp.zeros_like(ffn_rows))
    gate = jnp.dot(rows_in, gate_weight, preferred_element_type=jnp.float32)
    up_part = jnp.dot(rows_in, up_weight, preferred_element_type=jnp.float32)
    hidden = (jax.nn.silu(gate) * up_part).astype(jnp.bfloat16)
    ffn_out = jnp.dot(hidden, down_weight, preferred_element_type=jnp.float32).astype(jnp.bfloat16)
    query_wide = queries.astype(jnp.float32)
    cache_wide = latent_cache.astype(jnp.float32)
    scores = jnp.einsum("rhe,rte->rht", query_wide, cache_wide) * score_scale
    positions = jnp.arange(CTX)
    valid = positions[None, None, :] < cache_lengths[:, None, None]
    scores = jnp.where(valid, scores, -1e30)
    peak = jnp.max(scores, axis=2, keepdims=True)
    expo = jnp.exp(scores - peak)
    probs = (expo / jnp.sum(expo, axis=2, keepdims=True)).astype(jnp.bfloat16)
    context = jnp.einsum("rht,rtl->rhl", probs.astype(jnp.float32), cache_wide[:, :, :LATENT]).astype(jnp.bfloat16)
    request_index = jnp.arange(SLOTS * N_RANK)
    request_live = (request_index % SLOTS) < live_requests[request_index // SLOTS]
    attn_latent = jnp.where(request_live[:, None, None], context, jnp.zeros_like(context))
    return ffn_out, attn_latent
```

```python
import functools

import jax
import jax.numpy as jnp
from jax import lax
from jax.experimental import pallas as pl
from jax.experimental.pallas import tpu as pltpu
from jax.sharding import PartitionSpec as P

MESH = pl.DeviceIdType.MESH
D, FF, ROWS, LATENT = 7168, 288, 16, 512
NX, NZ, NY = 4, 8, 4
GROUP = NX * ROWS
SLICE = D // NX
HALF = SLICE // 2
TILE = 128
CA = 26 * TILE
A0 = 13 * TILE
CB = D - CA
B0 = 15 * TILE
KCH = 1024
score_scale = 192.0 ** (-0.5)


def layout():
    names = {}

    def add(name, count):
        names[name] = len_box[0]
        len_box[0] += count

    len_box = [0]
    add("a1", 3)
    add("b1", 8)
    add("a2", 32)
    add("b2", 32)
    add("w1", 3)
    add("w2", 9)
    add("wc", 12)
    add("h", 24)
    add("r", 14)
    add("f", 6)
    return names, len_box[0]


SEM, NSEM = layout()


def kernel(
    counts, live, lengths, rows_in, wg_in, wu_in, wd_in, q_in, c_in, ffn_out, attn_out,
    xi, xb, wg, wu, wd, qb, cb, acc, hid, part, sbuf, rbuf, fs, fo, ssem, rsem, lsem,
):
    inst = lax.axis_index("inst")
    rank = lax.axis_index("rank")
    y, c = inst // 2, inst % 2
    x, z = rank // NZ, rank % NZ
    yhi, ylo = y // 2, y % 2

    def at_x(k):
        return (inst, ((x + NX + k) % NX) * NZ + z)

    def at_z(k):
        return (inst, x * NZ + (z + NZ + k) % NZ)

    def at_y(k):
        return (((y + NY + k) % NY) * 2 + c, rank)

    other = (y * 2 + (1 - c), rank)
    zp, zm, xp, xm = at_z(1), at_z(-1), at_x(1), at_x(-1)

    loads = [
        pltpu.make_async_copy(rows_in, xi, lsem.at[0]),
        pltpu.make_async_copy(q_in, qb, lsem.at[1]),
        pltpu.make_async_copy(c_in, cb, lsem.at[2]),
        pltpu.make_async_copy(wg_in, wg, lsem.at[3]),
        pltpu.make_async_copy(wu_in, wu, lsem.at[4]),
        pltpu.make_async_copy(
            wd_in.at[:, pl.ds(pl.multiple_of(x * SLICE, TILE), SLICE)],
            wd.at[pl.ds(pl.multiple_of(x * FF, 16), FF), :],
            lsem.at[5],
        ),
    ]
    loads[0].start()

    barrier = pltpu.get_barrier_semaphore()
    peers = [zp, zm, xp, xm, at_x(2), at_y(1), at_y(-1), at_y(2), other]
    for peer in peers:
        pl.semaphore_signal(barrier, inc=1, device_id=peer, device_id_type=MESH)
    for load in loads[1:]:
        load.start()
    loads[0].wait()
    mine = pl.ds(pl.multiple_of((z * NX + x) * ROWS, ROWS), ROWS)
    row_live = lax.broadcasted_iota(jnp.int32, (ROWS, 1), 0) < counts[rank]
    xb[mine, :] = jnp.where(row_live, xi[...], jnp.zeros_like(xi[...]))
    pl.semaphore_wait(barrier, len(peers))

    sent = []

    def send(src, dst, index, peer):
        copy = pltpu.make_async_remote_copy(
            src, dst, ssem.at[index], rsem.at[index], device_id=peer, device_id_type=MESH
        )
        copy.start()
        sent.append(copy)

    def recv(dst, index):
        pltpu.make_async_remote_copy(
            dst, dst, ssem.at[index], rsem.at[index], device_id=zp, device_id_type=MESH
        ).wait_recv()

    def block(dx, dz):
        at = ((z + NZ + dz) % NZ) * NX + (x + NX + dx) % NX
        return pl.ds(pl.multiple_of(at * ROWS, ROWS), ROWS)

    def group(dz):
        return pl.ds(pl.multiple_of(((z + NZ + dz) % NZ) * GROUP, GROUP), GROUP)

    full_a, half_a = pl.ds(0, CA), (pl.ds(0, A0), pl.ds(A0, CA - A0))
    full_b, half_b = pl.ds(CA, CB), (pl.ds(CA, B0), pl.ds(CA + B0, CB - B0))
    toward = (zp, zm)

    def a2_index(way, hop, j):
        return SEM["a2"] + (way * 4 + hop - 1) * 4 + j

    def b1_index(way, hop):
        return SEM["b1"] + way * 4 + hop - 1

    def a2_send(way, hop, j):
        sign = -1 if way == 0 else 1
        cols = full_a if hop < 4 else half_a[way]
        ref = xb.at[block(-j, sign * (hop - 1)), cols]
        send(ref, ref, a2_index(way, hop, j), toward[way])

    def a2_recv(way, hop, j):
        sign = -1 if way == 0 else 1
        cols = full_a if hop < 4 else half_a[way]
        recv(xb.at[block(-j, sign * hop), cols], a2_index(way, hop, j))

    def b1_send(way, hop):
        sign = -1 if way == 0 else 1
        cols = full_b if hop < 4 else half_b[way]
        ref = xb.at[block(0, sign * (hop - 1)), cols]
        send(ref, ref, b1_index(way, hop), toward[way])

    def b1_recv(way, hop):
        sign = -1 if way == 0 else 1
        cols = full_b if hop < 4 else half_b[way]
        recv(xb.at[block(0, sign * hop), cols], b1_index(way, hop))

    def b2_index(dz, kind):
        return SEM["b2"] + (dz % NZ) * 4 + kind

    def b2_send(dz):
        ref = xb.at[block(0, dz), full_b]
        send(ref, ref, b2_index(dz, 0), xp)
        send(ref, ref, b2_index(dz, 1), xm)

    def b2_pass(dz):
        recv(xb.at[block(-1, dz), full_b], b2_index(dz, 0))
        ref = xb.at[block(-1, dz), half_b[0]]
        send(ref, ref, b2_index(dz, 2), xp)
        recv(xb.at[block(1, dz), full_b], b2_index(dz, 1))
        ref = xb.at[block(1, dz), half_b[1]]
        send(ref, ref, b2_index(dz, 3), xm)

    def b2_last(dz):
        recv(xb.at[block(-2, dz), half_b[0]], b2_index(dz, 2))
        recv(xb.at[block(2, dz), half_b[1]], b2_index(dz, 3))

    def wd_piece(xs, yy, start, count):
        row = xs * FF + (yy // 2) * 144 + start
        col = (yy % 2) * HALF
        return wd.at[pl.ds(pl.multiple_of(row, 16), count), pl.ds(pl.multiple_of(col, TILE), HALF)]

    def w1_send(k):
        to = (x + k) % NX
        src = wd_in.at[
            pl.ds(pl.multiple_of(yhi * 144 + c * 64, 16), 80),
            pl.ds(pl.multiple_of(to * SLICE + ylo * HALF, TILE), HALF),
        ]
        send(src, wd_piece(x, y, c * 64, 80), SEM["w1"] + k - 1, at_x(k))

    def wc_send(k, m):
        ref = wd_piece((x + NX - k) % NX, (y + NY - m) % NY, c * 80, 64)
        send(ref, ref, SEM["wc"] + (k - 1) * 4 + m, other)

    def w1_pass(k):
        ref = wd_piece((x + NX - k) % NX, y, c * 64, 80)
        recv(ref, SEM["w1"] + k - 1)
        for m in (1, 3, 2):
            send(ref, ref, SEM["w2"] + (k - 1) * 3 + m - 1, at_y(m))
        wc_send(k, 0)

    def w2_pass(k, m):
        ref = wd_piece((x + NX - k) % NX, (y + NY - m) % NY, c * 64, 80)
        recv(ref, SEM["w2"] + (k - 1) * 3 + m - 1)
        wc_send(k, m)

    def wc_recv(k, m):
        ref = wd_piece((x + NX - k) % NX, (y + NY - m) % NY, (1 - c) * 80, 64)
        recv(ref, SEM["wc"] + (k - 1) * 4 + m)

    pieces = []

    def tick(count=1):
        for _ in range(count):
            if pieces:
                pieces.pop(0)()

    def drain():
        while pieces:
            pieces.pop(0)()

    def attend(slot):
        keys = cb[slot]
        scores = lax.dot_general(
            qb[slot], keys, (((1,), (1,)), ((), ())), preferred_element_type=jnp.float32
        ) * score_scale
        places = lax.broadcasted_iota(jnp.int32, scores.shape, 1)
        scores = jnp.where(places < lengths[rank * 4 + slot], scores, -1e30)
        expo = jnp.exp(scores - jnp.max(scores, axis=1, keepdims=True))
        probs = (expo / jnp.sum(expo, axis=1, keepdims=True)).astype(jnp.bfloat16)
        value = jnp.dot(probs, keys[:, :LATENT], preferred_element_type=jnp.float32)
        keep = jnp.full((1, 1), slot, jnp.int32) < live[rank]
        attn_out[slot] = jnp.where(keep, value, 0.0).astype(jnp.bfloat16)

    def up_piece(pair, k):
        cols = pl.ds(k * KCH, KCH)
        rows = jnp.concatenate([xb[group(dz), cols] for dz in pair], axis=0)
        for which, weight in enumerate((wg, wu)):
            term = jnp.dot(rows, weight[cols, :], preferred_element_type=jnp.float32)
            if k == 0:
                acc[which] = term
            else:
                acc[which] += term

    def h_index(dz, k):
        return SEM["h"] + (dz % NZ) * 3 + k - 1

    def hidden_piece(pair):
        gate, up = acc[0], acc[1]
        value = (gate / (1.0 + jnp.exp(-gate)) * up).astype(jnp.bfloat16)
        for i, dz in enumerate(pair):
            hid[x, group(dz), :] = value[i * GROUP:(i + 1) * GROUP]
        for dz in pair:
            ref = hid.at[x, group(dz), :]
            for k in (1, 3, 2):
                send(ref, ref, h_index(dz, k), at_x(k))

    def hidden_wait(pair):
        for dz in pair:
            for k in (1, 3, 2):
                recv(hid.at[(x + NX - k) % NX, group(dz), :], h_index(dz, k))

    def down_piece(pair, n):
        cols = pl.ds(n * 256, 256)
        total = None
        for xs in range(NX):
            rows = jnp.concatenate([hid[xs, group(dz), :] for dz in pair], axis=0)
            term = jnp.dot(
                rows, wd[xs * FF:(xs + 1) * FF, cols], preferred_element_type=jnp.float32
            )
            total = term if total is None else total + term
        for i, dz in enumerate(pair):
            part[group(dz), cols] = total[i * GROUP:(i + 1) * GROUP]

    def queue_up(pair):
        for k in range(D // KCH):
            pieces.append(functools.partial(up_piece, pair, k))
        pieces.append(functools.partial(hidden_piece, pair))

    def queue_down(pair):
        pieces.append(functools.partial(hidden_wait, pair))
        for n in range(SLICE // 256):
            pieces.append(functools.partial(down_piece, pair, n))

    half_cols = (pl.ds(0, HALF), pl.ds(HALF, HALF))

    def ring_step(step):
        for way in range(2):
            sign = -1 if way == 0 else 1
            value = part[group(sign * (1 + step)), half_cols[way]]
            if step > 0:
                recv(rbuf.at[way, step - 1], SEM["r"] + way * 7 + step - 1)
                value = value + rbuf[way, step - 1].astype(jnp.float32)
            sbuf[way, step] = value.astype(jnp.bfloat16)
            send(sbuf.at[way, step], rbuf.at[way, step], SEM["r"] + way * 7 + step, toward[way])

    for k in (1, 3, 2):
        ref = xb.at[mine, full_a]
        send(ref, ref, SEM["a1"] + k - 1, at_x(k))
    for way in range(2):
        b1_send(way, 1)
        a2_send(way, 1, 0)
    b2_send(0)
    for k in (1, 3, 2):
        w1_send(k)
    loads[1].wait()
    loads[2].wait()
    attend(0)
    for k in (1, 3, 2):
        recv(xb.at[block(-k, 0), full_a], SEM["a1"] + k - 1)
        for way in range(2):
            a2_send(way, 1, k)
    b2_pass(0)
    attend(1)
    for k in (1, 3, 2):
        w1_pass(k)

    pieces.append(functools.partial(attend, 2))
    pieces.append(functools.partial(attend, 3))

    for hop in (1, 2, 3):
        for way in range(2):
            sign = -1 if way == 0 else 1
            b1_recv(way, hop)
            b1_send(way, hop + 1)
            if hop < 4:
                b2_send(sign * hop)
            tick()
        for j in (0, 1, 3, 2):
            for way in range(2):
                a2_recv(way, hop, j)
                a2_send(way, hop + 1, j)
            tick()
            if hop == 1 and j != 0:
                for m in (1, 3, 2):
                    w2_pass(j, m)
        for way in range(2):
            sign = -1 if way == 0 else 1
            b2_pass(sign * hop)
            tick()
        if hop == 1:
            b2_last(0)
            loads[3].wait()
            loads[4].wait()
            loads[5].wait()
            for k in (1, 2, 3):
                for m in range(4):
                    wc_recv(k, m)
        for way in range(2):
            b2_last((-1 if way == 0 else 1) * hop)
        drain()
        queue_up((-hop, hop))
        if hop > 1:
            queue_down((1 - hop, hop - 1))

    for way in range(2):
        b1_recv(way, 4)
    b2_send(4)
    tick(4)
    for j in (0, 1, 3, 2):
        for way in range(2):
            a2_recv(way, 4, j)
        tick()
    b2_pass(4)
    tick(4)
    b2_last(4)
    drain()
    ring_step(0)
    queue_up((0, 4))
    drain()
    queue_down((-3, 3))
    drain()
    ring_step(1)
    queue_down((0, 4))
    drain()
    for step in range(2, 7):
        ring_step(step)

    for way in range(2):
        recv(rbuf.at[way, 6], SEM["r"] + way * 7 + 6)
        value = part[group(0), half_cols[way]] + rbuf[way, 6].astype(jnp.float32)
        fs[way] = value.astype(jnp.bfloat16)
        cols = pl.ds(pl.multiple_of(x * SLICE + way * HALF, TILE), HALF)
        for k in (1, 3, 2):
            to = (x + k) % NX
            send(
                fs.at[way, pl.ds(pl.multiple_of(to * ROWS, ROWS), ROWS), :],
                fo.at[:, cols], SEM["f"] + way * 3 + k - 1, at_x(k),
            )
        fo[:, cols] = fs[way, pl.ds(pl.multiple_of(x * ROWS, ROWS), ROWS), :]
    for copy in sent:
        copy.wait_send()
    for way in range(2):
        for k in (1, 3, 2):
            cols = pl.ds(pl.multiple_of(((x + NX - k) % NX) * SLICE + way * HALF, TILE), HALF)
            recv(fo.at[:, cols], SEM["f"] + way * 3 + k - 1)
    ffn_out[...] = fo[...]


def body(rows, counts, gate, up, down, queries, cache, live, lengths):
    bf16, f32 = jnp.bfloat16, jnp.float32
    smem = pl.BlockSpec(memory_space=pltpu.SMEM)
    hbm = pl.BlockSpec(memory_space=pl.ANY)
    vmem = pl.BlockSpec(memory_space=pltpu.VMEM)
    return pl.pallas_call(
        kernel,
        out_shape=(
            jax.ShapeDtypeStruct((ROWS, D), bf16),
            jax.ShapeDtypeStruct((4, 64, LATENT), bf16),
        ),
        in_specs=[smem] * 3 + [hbm] * 6,
        out_specs=(vmem, vmem),
        scratch_shapes=[
            pltpu.VMEM((ROWS, D), bf16),
            pltpu.VMEM((NZ * GROUP, D), bf16),
            pltpu.VMEM((D, FF), bf16),
            pltpu.VMEM((D, FF), bf16),
            pltpu.VMEM((NX * FF, SLICE), bf16),
            pltpu.VMEM((4, 64, 576), bf16),
            pltpu.VMEM((4, 64, 576), bf16),
            pltpu.VMEM((2, 2 * GROUP, FF), f32),
            pltpu.VMEM((NX, NZ * GROUP, FF), bf16),
            pltpu.VMEM((NZ * GROUP, SLICE), f32),
            pltpu.VMEM((2, 7, GROUP, HALF), bf16),
            pltpu.VMEM((2, 7, GROUP, HALF), bf16),
            pltpu.VMEM((2, GROUP, HALF), bf16),
            pltpu.VMEM((ROWS, D), bf16),
            pltpu.SemaphoreType.DMA((NSEM,)),
            pltpu.SemaphoreType.DMA((NSEM,)),
            pltpu.SemaphoreType.DMA((6,)),
        ],
        compiler_params=pltpu.CompilerParams(
            collective_id=1, has_side_effects=True, vmem_limit_bytes=56 * 2**20
        ),
        cost_estimate=pl.CostEstimate(
            flops=2 * 512 * D * FF * 3, bytes_accessed=16 * 2**20, transcendentals=512 * FF
        ),
    )(counts, live, lengths, rows, gate, up, down, queries, cache)


def solution(mesh):
    placed = (
        P(("inst", "rank"), None),
        P("inst"),
        P(None, "rank"),
        P(None, "rank"),
        P("rank", None),
        P(("inst", "rank"), None, None),
        P(("inst", "rank"), None, None),
        P("inst"),
        P("inst"),
    )
    return jax.shard_map(
        body,
        mesh=mesh,
        in_specs=placed,
        out_specs=(P(("inst", "rank"), None), P(("inst", "rank"), None, None)),
        check_vma=False,
    )
```

```python
import functools

import jax
import jax.numpy as jnp
from jax import lax
from jax.experimental import pallas as pl
from jax.experimental.pallas import tpu as pltpu
from jax.sharding import PartitionSpec as P

MESH = pl.DeviceIdType.MESH
D, FF, ROWS, LATENT = 7168, 288, 16, 512
NX, NZ, NY = 4, 8, 4
GROUP = NX * ROWS
SLICE = D // NX
HALF = SLICE // 2
TILE = 128
CA = 30 * TILE
A0 = 15 * TILE
CB = D - CA
B0 = 13 * TILE
KCH = 1024
SUBS, SUB = 4, 16
score_scale = 192.0 ** (-0.5)


def layout():
    names = {}

    def add(name, count):
        names[name] = len_box[0]
        len_box[0] += count

    len_box = [0]
    add("a1", 3)
    add("b1", 8)
    add("a2", 32)
    add("b2", 32)
    add("w1", 3)
    add("w2", 9)
    add("wc", 12)
    add("h", 24)
    add("ht", 24)
    add("r", 56)
    add("f", 6)
    return names, len_box[0]


SEM, NSEM = layout()


def kernel(
    counts, live, lengths, rows_in, wg_in, wu_in, wd_in, q_in, c_in, ffn_out, attn_out,
    xi, xb, wgu, wd, qb, cb, acc, hid, tail, rest, part, sbuf, rbuf, fs, fo, ssem, rsem, lsem,
):
    inst = lax.axis_index("inst")
    rank = lax.axis_index("rank")
    y, c = inst // 2, inst % 2
    x, z = rank // NZ, rank % NZ
    yhi, ylo = y // 2, y % 2

    def at_x(k):
        return (inst, ((x + NX + k) % NX) * NZ + z)

    def at_z(k):
        return (inst, x * NZ + (z + NZ + k) % NZ)

    def at_y(k):
        return (((y + NY + k) % NY) * 2 + c, rank)

    other = (y * 2 + (1 - c), rank)
    zp, zm, xp, xm = at_z(1), at_z(-1), at_x(1), at_x(-1)

    loads = [
        pltpu.make_async_copy(rows_in, xi, lsem.at[0]),
        pltpu.make_async_copy(q_in, qb, lsem.at[1]),
        pltpu.make_async_copy(c_in, cb, lsem.at[2]),
        pltpu.make_async_copy(wg_in, wgu.at[0:FF, :], lsem.at[3]),
        pltpu.make_async_copy(wu_in, wgu.at[FF:2 * FF, :], lsem.at[4]),
        pltpu.make_async_copy(
            wd_in.at[:, pl.ds(pl.multiple_of(x * SLICE, TILE), SLICE)],
            wd.at[pl.ds(pl.multiple_of(x * FF, 16), FF), :],
            lsem.at[5],
        ),
    ]
    loads[0].start()

    barrier = pltpu.get_barrier_semaphore()
    peers = [zp, zm, xp, xm, at_x(2), at_y(1), at_y(-1), at_y(2), other]
    for peer in peers:
        pl.semaphore_signal(barrier, inc=1, device_id=peer, device_id_type=MESH)
    for load in loads[1:]:
        load.start()
    loads[0].wait()
    mine = pl.ds(pl.multiple_of((z * NX + x) * ROWS, ROWS), ROWS)
    row_live = lax.broadcasted_iota(jnp.int32, (ROWS, 1), 0) < counts[rank]
    xb[mine, :] = jnp.where(row_live, xi[...], jnp.zeros_like(xi[...]))
    pl.semaphore_wait(barrier, len(peers))

    sent = []

    def send(src, dst, index, peer):
        copy = pltpu.make_async_remote_copy(
            src, dst, ssem.at[index], rsem.at[index], device_id=peer, device_id_type=MESH
        )
        copy.start()
        sent.append(copy)

    def recv(dst, index):
        pltpu.make_async_remote_copy(
            dst, dst, ssem.at[index], rsem.at[index], device_id=zp, device_id_type=MESH
        ).wait_recv()

    def block(dx, dz):
        at = ((z + NZ + dz) % NZ) * NX + (x + NX + dx) % NX
        return pl.ds(pl.multiple_of(at * ROWS, ROWS), ROWS)

    def group(dz):
        return pl.ds(pl.multiple_of(((z + NZ + dz) % NZ) * GROUP, GROUP), GROUP)

    full_a, half_a = pl.ds(0, CA), (pl.ds(0, A0), pl.ds(A0, CA - A0))
    full_b, half_b = pl.ds(CA, CB), (pl.ds(CA, B0), pl.ds(CA + B0, CB - B0))
    toward = (zp, zm)

    def a2_index(way, hop, j):
        return SEM["a2"] + (way * 4 + hop - 1) * 4 + j

    def b1_index(way, hop):
        return SEM["b1"] + way * 4 + hop - 1

    def a2_send(way, hop, j):
        sign = -1 if way == 0 else 1
        cols = full_a if hop < 4 else half_a[way]
        ref = xb.at[block(-j, sign * (hop - 1)), cols]
        send(ref, ref, a2_index(way, hop, j), toward[way])

    def a2_recv(way, hop, j):
        sign = -1 if way == 0 else 1
        cols = full_a if hop < 4 else half_a[way]
        recv(xb.at[block(-j, sign * hop), cols], a2_index(way, hop, j))

    def b1_send(way, hop):
        sign = -1 if way == 0 else 1
        cols = full_b if hop < 4 else half_b[way]
        ref = xb.at[block(0, sign * (hop - 1)), cols]
        send(ref, ref, b1_index(way, hop), toward[way])

    def b1_recv(way, hop):
        sign = -1 if way == 0 else 1
        cols = full_b if hop < 4 else half_b[way]
        recv(xb.at[block(0, sign * hop), cols], b1_index(way, hop))

    def b2_index(dz, kind):
        return SEM["b2"] + (dz % NZ) * 4 + kind

    def b2_send(dz):
        ref = xb.at[block(0, dz), full_b]
        send(ref, ref, b2_index(dz, 0), xp)
        send(ref, ref, b2_index(dz, 1), xm)

    def b2_pass(dz):
        recv(xb.at[block(-1, dz), full_b], b2_index(dz, 0))
        ref = xb.at[block(-1, dz), half_b[0]]
        send(ref, ref, b2_index(dz, 2), xp)
        recv(xb.at[block(1, dz), full_b], b2_index(dz, 1))
        ref = xb.at[block(1, dz), half_b[1]]
        send(ref, ref, b2_index(dz, 3), xm)

    def b2_last(dz):
        recv(xb.at[block(-2, dz), half_b[0]], b2_index(dz, 2))
        recv(xb.at[block(2, dz), half_b[1]], b2_index(dz, 3))

    def wd_piece(xs, yy, start, count):
        row = xs * FF + (yy // 2) * 144 + start
        col = (yy % 2) * HALF
        return wd.at[pl.ds(pl.multiple_of(row, 16), count), pl.ds(pl.multiple_of(col, TILE), HALF)]

    def w1_send(k):
        to = (x + k) % NX
        src = wd_in.at[
            pl.ds(pl.multiple_of(yhi * 144 + c * 64, 16), 80),
            pl.ds(pl.multiple_of(to * SLICE + ylo * HALF, TILE), HALF),
        ]
        send(src, wd_piece(x, y, c * 64, 80), SEM["w1"] + k - 1, at_x(k))

    def wc_send(k, m):
        ref = wd_piece((x + NX - k) % NX, (y + NY - m) % NY, c * 80, 64)
        send(ref, ref, SEM["wc"] + (k - 1) * 4 + m, other)

    def w1_pass(k):
        ref = wd_piece((x + NX - k) % NX, y, c * 64, 80)
        recv(ref, SEM["w1"] + k - 1)
        for m in (1, 3, 2):
            send(ref, ref, SEM["w2"] + (k - 1) * 3 + m - 1, at_y(m))
        wc_send(k, 0)

    def w2_pass(k, m):
        ref = wd_piece((x + NX - k) % NX, (y + NY - m) % NY, c * 64, 80)
        recv(ref, SEM["w2"] + (k - 1) * 3 + m - 1)
        wc_send(k, m)

    def wc_recv(k, m):
        ref = wd_piece((x + NX - k) % NX, (y + NY - m) % NY, (1 - c) * 80, 64)
        recv(ref, SEM["wc"] + (k - 1) * 4 + m)

    pieces = []

    def tick(count=1):
        for _ in range(count):
            if pieces:
                pieces.pop(0)()

    def drain():
        while pieces:
            pieces.pop(0)()

    def attend(slot):
        keys = cb[slot]
        scores = lax.dot_general(
            qb[slot], keys, (((1,), (1,)), ((), ())), preferred_element_type=jnp.float32
        ) * score_scale
        places = lax.broadcasted_iota(jnp.int32, scores.shape, 1)
        scores = jnp.where(places < lengths[rank * 4 + slot], scores, -1e30)
        expo = jnp.exp(scores - jnp.max(scores, axis=1, keepdims=True))
        probs = (expo / jnp.sum(expo, axis=1, keepdims=True)).astype(jnp.bfloat16)
        value = jnp.dot(probs, keys[:, :LATENT], preferred_element_type=jnp.float32)
        keep = jnp.full((1, 1), slot, jnp.int32) < live[rank]
        attn_out[slot] = jnp.where(keep, value, 0.0).astype(jnp.bfloat16)

    def up_piece(pair, k):
        cols = pl.ds(k * KCH, KCH)
        rows = jnp.concatenate([xb[group(dz), cols] for dz in pair], axis=0)
        for which in range(2):
            term = lax.dot_general(
                rows, wgu[which * FF:(which + 1) * FF, cols], (((1,), (1,)), ((), ())),
                preferred_element_type=jnp.float32,
            )
            size = len(pair) * GROUP
            if k == 0:
                acc[which, :size] = term
            else:
                acc[which, :size] += term

    def h_send(dz, part_of):
        for k in (1, 3, 2):
            at = ((dz % NZ) * 3 + k - 1)
            if part_of == 0:
                ref = hid.at[x, group(dz), :]
                send(ref, ref, SEM["h"] + at, at_x(k))
            else:
                ref = tail.at[x, quarter(dz), :]
                send(ref, ref, SEM["ht"] + at, at_x(k))

    def quarter(dz):
        return pl.ds(pl.multiple_of(((z + NZ + dz) % NZ) * ROWS, ROWS), ROWS)

    def hidden_piece(pair):
        size = len(pair) * GROUP
        gate, up = acc[0, :size], acc[1, :size]
        value = (gate / (1.0 + jnp.exp(-gate)) * up).astype(jnp.bfloat16)
        for i, dz in enumerate(pair):
            rows = value[i * GROUP:(i + 1) * GROUP]
            hid[x, group(dz), :] = rows[:, :256]
            tail[x, quarter(dz), :] = jnp.concatenate(
                [rows[n * ROWS:(n + 1) * ROWS, 256:] for n in range(4)], axis=1
            )
            h_send(dz, 0)
            h_send(dz, 1)

    def hidden_wait(pair):
        for dz in pair:
            for k in (1, 3, 2):
                at = ((dz % NZ) * 3 + k - 1)
                recv(hid.at[(x + NX - k) % NX, group(dz), :], SEM["h"] + at)
                recv(tail.at[(x + NX - k) % NX, quarter(dz), :], SEM["ht"] + at)
        for i, dz in enumerate(pair):
            packed = [tail[xs, quarter(dz), :] for xs in range(NX)]
            rest[i * GROUP:(i + 1) * GROUP, :] = jnp.concatenate(
                [
                    jnp.concatenate([p[:, n * 32:(n + 1) * 32] for p in packed], axis=1)
                    for n in range(4)
                ],
                axis=0,
            )

    def down_piece(pair, n):
        cols = pl.ds(n * 256, 256)
        size = len(pair) * GROUP
        lower = jnp.concatenate([wd[xs * FF + 256:(xs + 1) * FF, cols] for xs in range(NX)], axis=0)
        total = jnp.dot(rest[:size, :], lower, preferred_element_type=jnp.float32)
        for xs in range(NX):
            rows = jnp.concatenate([hid[xs, group(dz), :] for dz in pair], axis=0)
            total += jnp.dot(
                rows, wd[xs * FF:xs * FF + 256, cols], preferred_element_type=jnp.float32
            )
        for i, dz in enumerate(pair):
            part[group(dz), cols] = total[i * GROUP:(i + 1) * GROUP]

    def queue_up(pair):
        for k in range(D // KCH):
            pieces.append(functools.partial(up_piece, pair, k))
        pieces.append(functools.partial(hidden_piece, pair))

    def queue_down(pair):
        pieces.append(functools.partial(hidden_wait, pair))
        for n in range(SLICE // 256):
            pieces.append(functools.partial(down_piece, pair, n))

    half_cols = (pl.ds(0, HALF), pl.ds(HALF, HALF))

    def ring_step(step):
        for sub in range(SUBS):
            rows = pl.ds(sub * SUB, SUB)
            for way in range(2):
                index = SEM["r"] + (way * 7 + step) * SUBS + sub
                dz = (-1 if way == 0 else 1) * (1 + step)
                at = ((z + NZ + dz) % NZ) * GROUP + sub * SUB
                value = part[pl.ds(pl.multiple_of(at, SUB), SUB), half_cols[way]]
                if step > 0:
                    recv(rbuf.at[way, step - 1, rows], index - SUBS)
                    value = value + rbuf[way, step - 1, rows].astype(jnp.float32)
                sbuf[way, step, rows] = value.astype(jnp.bfloat16)
                send(sbuf.at[way, step, rows], rbuf.at[way, step, rows], index, toward[way])

    ways = ((0, -1), (1, 1))

    def b1(hop):
        for way, sign in ways:
            b1_recv(way, hop)
            if hop < 4:
                b1_send(way, hop + 1)
                b2_send(sign * hop)
        if hop == 4:
            b2_send(4)

    def a2(hop, j):
        for way, sign in ways:
            a2_recv(way, hop, j)
            if hop < 4:
                a2_send(way, hop + 1, j)

    def last(hop):
        for way, sign in ways[:1 if hop in (0, 4) else 2]:
            b2_last(sign * hop)

    def a1(k):
        recv(xb.at[block(-k, 0), full_a], SEM["a1"] + k - 1)
        for way in range(2):
            a2_send(way, 1, k)

    for k in (1, 3, 2):
        ref = xb.at[mine, full_a]
        send(ref, ref, SEM["a1"] + k - 1, at_x(k))
    for way, sign in ways:
        b1_send(way, 1)
        a2_send(way, 1, 0)
    b2_send(0)
    loads[1].wait()
    loads[2].wait()
    attend(0)
    a1(1)
    a1(3)
    b1(1)
    a1(2)
    for k in (1, 3, 2):
        w1_send(k)
    a2(1, 0)
    b2_pass(0)
    attend(1)
    a2(1, 1)
    attend(2)
    a2(1, 3)
    b2_pass(-1)
    attend(3)
    a2(1, 2)
    b2_pass(1)
    for load in loads[3:]:
        load.wait()

    b1(2)
    a2(2, 0)
    last(0)
    a2(2, 1)
    last(1)
    queue_up((-1, 0, 1))
    tick(2)
    w1_pass(1)
    a2(2, 3)
    tick(2)
    b2_pass(-2)
    w1_pass(3)
    a2(2, 2)
    tick(2)
    b2_pass(2)
    w1_pass(2)
    b1(3)
    drain()
    a2(3, 0)
    a2(3, 1)
    last(2)
    queue_up((-2, 2))
    tick(2)
    for m in (1, 3, 2):
        w2_pass(1, m)
    a2(3, 3)
    tick(2)
    b2_pass(-3)
    for m in (1, 3, 2):
        w2_pass(3, m)
    a2(3, 2)
    tick(2)
    b2_pass(3)
    for m in (1, 3, 2):
        w2_pass(2, m)
    drain()
    b1(4)
    for k in (1, 2, 3):
        for m in range(4):
            wc_recv(k, m)
    queue_down((-1, 0, 1))
    drain()
    ring_step(0)
    a2(4, 0)
    last(3)
    queue_up((-3, 3))
    tick(4)
    a2(4, 1)
    b2_pass(4)
    drain()
    queue_down((-2, 2))
    drain()
    ring_step(1)
    a2(4, 3)
    a2(4, 2)
    for k in range(3):
        up_piece((4,), k)
    last(4)
    for k in range(3, D // KCH):
        up_piece((4,), k)
    hidden_piece((4,))
    queue_down((-3, 3))
    drain()
    ring_step(2)
    queue_down((4,))
    drain()
    for step in range(3, 7):
        ring_step(step)

    for way in range(2):
        for sub in range(SUBS):
            recv(rbuf.at[way, 6, pl.ds(sub * SUB, SUB)], SEM["r"] + (way * 7 + 6) * SUBS + sub)
        value = part[group(0), half_cols[way]] + rbuf[way, 6].astype(jnp.float32)
        fs[way] = value.astype(jnp.bfloat16)
        cols = pl.ds(pl.multiple_of(x * SLICE + way * HALF, TILE), HALF)
        for k in (1, 3, 2):
            to = (x + k) % NX
            send(
                fs.at[way, pl.ds(pl.multiple_of(to * ROWS, ROWS), ROWS), :],
                fo.at[:, cols], SEM["f"] + way * 3 + k - 1, at_x(k),
            )
        fo[:, cols] = fs[way, pl.ds(pl.multiple_of(x * ROWS, ROWS), ROWS), :]
    for copy in sent:
        copy.wait_send()
    for way in range(2):
        for k in (1, 3, 2):
            cols = pl.ds(pl.multiple_of(((x + NX - k) % NX) * SLICE + way * HALF, TILE), HALF)
            recv(fo.at[:, cols], SEM["f"] + way * 3 + k - 1)
    ffn_out[...] = fo[...]


def body(rows, counts, gate, up, down, queries, cache, live, lengths):
    bf16, f32 = jnp.bfloat16, jnp.float32
    smem = pl.BlockSpec(memory_space=pltpu.SMEM)
    hbm = pl.BlockSpec(memory_space=pl.ANY)
    vmem = pl.BlockSpec(memory_space=pltpu.VMEM)
    return pl.pallas_call(
        kernel,
        out_shape=(
            jax.ShapeDtypeStruct((ROWS, D), bf16),
            jax.ShapeDtypeStruct((4, 64, LATENT), bf16),
        ),
        in_specs=[smem] * 3 + [hbm] * 6,
        out_specs=(vmem, vmem),
        scratch_shapes=[
            pltpu.VMEM((ROWS, D), bf16),
            pltpu.VMEM((NZ * GROUP, D), bf16),
            pltpu.VMEM((2 * FF, D), bf16),
            pltpu.VMEM((NX * FF, SLICE), bf16),
            pltpu.VMEM((4, 64, 576), bf16),
            pltpu.VMEM((4, 64, 576), bf16),
            pltpu.VMEM((2, 3 * GROUP, FF), f32),
            pltpu.VMEM((NX, NZ * GROUP, 256), bf16),
            pltpu.VMEM((NX, NZ * ROWS, 128), bf16),
            pltpu.VMEM((3 * GROUP, 128), bf16),
            pltpu.VMEM((NZ * GROUP, SLICE), f32),
            pltpu.VMEM((2, 7, GROUP, HALF), bf16),
            pltpu.VMEM((2, 7, GROUP, HALF), bf16),
            pltpu.VMEM((2, GROUP, HALF), bf16),
            pltpu.VMEM((ROWS, D), bf16),
            pltpu.SemaphoreType.DMA((NSEM,)),
            pltpu.SemaphoreType.DMA((NSEM,)),
            pltpu.SemaphoreType.DMA((6,)),
        ],
        compiler_params=pltpu.CompilerParams(
            collective_id=1, has_side_effects=True, vmem_limit_bytes=56 * 2**20
        ),
        cost_estimate=pl.CostEstimate(
            flops=2 * 512 * D * FF * 3, bytes_accessed=16 * 2**20, transcendentals=512 * FF
        ),
    )(counts, live, lengths, rows, gate.T, up.T, down, queries, cache)


def solution(mesh):
    placed = (
        P(("inst", "rank"), None),
        P("inst"),
        P(None, "rank"),
        P(None, "rank"),
        P("rank", None),
        P(("inst", "rank"), None, None),
        P(("inst", "rank"), None, None),
        P("inst"),
        P("inst"),
    )
    return jax.shard_map(
        body,
        mesh=mesh,
        in_specs=placed,
        out_specs=(P(("inst", "rank"), None), P(("inst", "rank"), None, None)),
        check_vma=False,
    )
```

```python
import functools

import jax
import jax.numpy as jnp
from jax import lax
from jax.experimental import pallas as pl
from jax.experimental.pallas import tpu as pltpu
from jax.sharding import PartitionSpec as P

MESH = pl.DeviceIdType.MESH
D, FF, ROWS, LATENT = 7168, 288, 16, 512
NX, NZ, NY = 4, 8, 4
GROUP = NX * ROWS
SLICE = D // NX
HALF = SLICE // 2
TILE = 128
CA = 30 * TILE
A0 = 15 * TILE
CB = D - CA
B0 = 13 * TILE
KCH = 1792
SUBS, SUB = 4, 16
score_scale = 192.0 ** (-0.5)


def layout():
    names = {}

    def add(name, count):
        names[name] = len_box[0]
        len_box[0] += count

    len_box = [0]
    add("a1", 3)
    add("b1", 8)
    add("a2", 32)
    add("b2", 32)
    add("w1", 3)
    add("w2", 9)
    add("wc", 12)
    add("h", 24)
    add("ht", 24)
    add("r", 56)
    add("f", 8)
    add("n", 3)
    return names, len_box[0]


SEM, NSEM = layout()


def kernel(
    counts, live, lengths, rows_in, wg_in, wu_in, wd_in, q_in, c_in, ffn_out, attn_out,
    xi, xb, wgu, wgt, wd, qb, cb, acc, hid, tail, rest, part, sbuf, rbuf, near, own, fin, ssem, rsem, lsem,
):
    inst = lax.axis_index("inst")
    rank = lax.axis_index("rank")
    y, c = inst // 2, inst % 2
    x, z = rank // NZ, rank % NZ
    yhi, ylo = y // 2, y % 2

    def at_x(k):
        return (inst, ((x + NX + k) % NX) * NZ + z)

    def at_z(k):
        return (inst, x * NZ + (z + NZ + k) % NZ)

    def at_y(k):
        return (((y + NY + k) % NY) * 2 + c, rank)

    other = (y * 2 + (1 - c), rank)
    zp, zm, xp, xm = at_z(1), at_z(-1), at_x(1), at_x(-1)

    def beside(way, k):
        return (inst, ((x + k) % NX) * NZ + (z + NZ + (1 if way == 0 else -1)) % NZ)


    loads = [
        pltpu.make_async_copy(rows_in, xi, lsem.at[0]),
        pltpu.make_async_copy(q_in, qb, lsem.at[1]),
        pltpu.make_async_copy(c_in, cb, lsem.at[2]),
        pltpu.make_async_copy(wg_in.at[0:256, :], wgu.at[0:256, :], lsem.at[3]),
        pltpu.make_async_copy(wu_in.at[0:256, :], wgu.at[256:512, :], lsem.at[4]),
        pltpu.make_async_copy(wg_in.at[256:288, :], wgu.at[512:544, :], lsem.at[6]),
        pltpu.make_async_copy(wu_in.at[256:288, :], wgu.at[544:576, :], lsem.at[7]),
        pltpu.make_async_copy(
            wd_in.at[:, pl.ds(pl.multiple_of(x * SLICE, TILE), SLICE)],
            wd.at[pl.ds(pl.multiple_of(x * FF, 16), FF), :],
            lsem.at[5],
        ),
    ]
    loads[0].start()

    barrier = pltpu.get_barrier_semaphore()
    peers = [zp, zm, xp, xm, at_x(2), at_y(1), at_y(-1), at_y(2), other]
    peers += [beside(way, k) for way in range(2) for k in (1, 2, 3)]
    for peer in peers:
        pl.semaphore_signal(barrier, inc=1, device_id=peer, device_id_type=MESH)
    for load in loads[1:]:
        load.start()
    loads[0].wait()
    mine = pl.ds(pl.multiple_of((z * NX + x) * ROWS, ROWS), ROWS)
    row_live = lax.broadcasted_iota(jnp.int32, (ROWS, 1), 0) < counts[rank]
    xb[mine, :] = jnp.where(row_live, xi[...], jnp.zeros_like(xi[...]))
    pl.semaphore_wait(barrier, len(peers))

    sent = []

    def send(src, dst, index, peer):
        copy = pltpu.make_async_remote_copy(
            src, dst, ssem.at[index], rsem.at[index], device_id=peer, device_id_type=MESH
        )
        copy.start()
        sent.append(copy)

    def recv(dst, index):
        pltpu.make_async_remote_copy(
            dst, dst, ssem.at[index], rsem.at[index], device_id=zp, device_id_type=MESH
        ).wait_recv()

    def block(dx, dz):
        at = ((z + NZ + dz) % NZ) * NX + (x + NX + dx) % NX
        return pl.ds(pl.multiple_of(at * ROWS, ROWS), ROWS)

    def group(dz):
        return pl.ds(pl.multiple_of(((z + NZ + dz) % NZ) * GROUP, GROUP), GROUP)

    full_a, half_a = pl.ds(0, CA), (pl.ds(0, A0), pl.ds(A0, CA - A0))
    full_b, half_b = pl.ds(CA, CB), (pl.ds(CA, B0), pl.ds(CA + B0, CB - B0))
    toward = (zp, zm)

    def a2_index(way, hop, j):
        return SEM["a2"] + (way * 4 + hop - 1) * 4 + j

    def b1_index(way, hop):
        return SEM["b1"] + way * 4 + hop - 1

    def a2_send(way, hop, j):
        sign = -1 if way == 0 else 1
        cols = full_a if hop < 4 else half_a[way]
        ref = xb.at[block(-j, sign * (hop - 1)), cols]
        send(ref, ref, a2_index(way, hop, j), toward[way])

    def a2_recv(way, hop, j):
        sign = -1 if way == 0 else 1
        cols = full_a if hop < 4 else half_a[way]
        recv(xb.at[block(-j, sign * hop), cols], a2_index(way, hop, j))

    def b1_send(way, hop):
        sign = -1 if way == 0 else 1
        cols = full_b if hop < 4 else half_b[way]
        ref = xb.at[block(0, sign * (hop - 1)), cols]
        send(ref, ref, b1_index(way, hop), toward[way])

    def b1_recv(way, hop):
        sign = -1 if way == 0 else 1
        cols = full_b if hop < 4 else half_b[way]
        recv(xb.at[block(0, sign * hop), cols], b1_index(way, hop))

    def b2_index(dz, kind):
        return SEM["b2"] + (dz % NZ) * 4 + kind

    def b2_send(dz):
        ref = xb.at[block(0, dz), full_b]
        send(ref, ref, b2_index(dz, 0), xp)
        send(ref, ref, b2_index(dz, 1), xm)
        if dz == 4:
            send(ref, ref, b2_index(dz, 2), at_x(2))

    def b2_pass(dz):
        recv(xb.at[block(-1, dz), full_b], b2_index(dz, 0))
        ref = xb.at[block(-1, dz), half_b[0]]
        send(ref, ref, b2_index(dz, 2), xp)
        recv(xb.at[block(1, dz), full_b], b2_index(dz, 1))
        ref = xb.at[block(1, dz), half_b[1]]
        send(ref, ref, b2_index(dz, 3), xm)

    def b2_far():
        for k, kind in ((1, 0), (3, 1), (2, 2)):
            recv(xb.at[block(-k, 4), full_b], b2_index(4, kind))

    def b2_last(dz):
        recv(xb.at[block(-2, dz), half_b[0]], b2_index(dz, 2))
        recv(xb.at[block(2, dz), half_b[1]], b2_index(dz, 3))

    def wd_piece(xs, yy, start, count):
        row = xs * FF + (yy // 2) * 144 + start
        col = (yy % 2) * HALF
        return wd.at[pl.ds(pl.multiple_of(row, 16), count), pl.ds(pl.multiple_of(col, TILE), HALF)]

    def w1_send(k):
        to = (x + k) % NX
        src = wd_in.at[
            pl.ds(pl.multiple_of(yhi * 144 + c * 64, 16), 80),
            pl.ds(pl.multiple_of(to * SLICE + ylo * HALF, TILE), HALF),
        ]
        send(src, wd_piece(x, y, c * 64, 80), SEM["w1"] + k - 1, at_x(k))

    def wc_send(k, m):
        ref = wd_piece((x + NX - k) % NX, (y + NY - m) % NY, c * 80, 64)
        send(ref, ref, SEM["wc"] + (k - 1) * 4 + m, other)

    def w1_pass(k):
        ref = wd_piece((x + NX - k) % NX, y, c * 64, 80)
        recv(ref, SEM["w1"] + k - 1)
        for m in (1, 3, 2):
            send(ref, ref, SEM["w2"] + (k - 1) * 3 + m - 1, at_y(m))
        wc_send(k, 0)

    def w2_pass(k, m):
        ref = wd_piece((x + NX - k) % NX, (y + NY - m) % NY, c * 64, 80)
        recv(ref, SEM["w2"] + (k - 1) * 3 + m - 1)
        wc_send(k, m)

    def wc_recv(k, m):
        ref = wd_piece((x + NX - k) % NX, (y + NY - m) % NY, (1 - c) * 80, 64)
        recv(ref, SEM["wc"] + (k - 1) * 4 + m)

    pieces = []

    def tick(count=1):
        for _ in range(count):
            if pieces:
                pieces.pop(0)()

    def drain():
        while pieces:
            pieces.pop(0)()

    def attend(slot):
        keys = cb[slot]
        scores = lax.dot_general(
            qb[slot], keys, (((1,), (1,)), ((), ())), preferred_element_type=jnp.float32
        ) * score_scale
        places = lax.broadcasted_iota(jnp.int32, scores.shape, 1)
        scores = jnp.where(places < lengths[rank * 4 + slot], scores, -1e30)
        expo = jnp.exp(scores - jnp.max(scores, axis=1, keepdims=True))
        probs = (expo / jnp.sum(expo, axis=1, keepdims=True)).astype(jnp.bfloat16)
        value = jnp.dot(probs, keys[:, :LATENT], preferred_element_type=jnp.float32)
        keep = jnp.full((1, 1), slot, jnp.int32) < live[rank]
        attn_out[slot] = jnp.where(keep, value, 0.0).astype(jnp.bfloat16)

    def turn_piece(k):
        cols = pl.ds(k * 512, 512)
        wgt[cols, :] = wgu[:, cols].T

    def up_piece(pair, k):
        cols = pl.ds(k * KCH, KCH)
        rows = jnp.concatenate([xb[group(dz), cols] for dz in pair], axis=0)
        term = jnp.dot(rows, wgt[cols, :], preferred_element_type=jnp.float32)
        size = len(pair) * GROUP
        if k == 0:
            acc[:size] = term
        else:
            acc[:size] += term

    def h_send(dz, part_of):
        for k in (1, 3, 2):
            at = ((dz % NZ) * 3 + k - 1)
            if part_of == 0:
                ref = hid.at[x, group(dz), :]
                send(ref, ref, SEM["h"] + at, at_x(k))
            else:
                ref = tail.at[x, quarter(dz), :]
                send(ref, ref, SEM["ht"] + at, at_x(k))

    def quarter(dz):
        return pl.ds(pl.multiple_of(((z + NZ + dz) % NZ) * ROWS, ROWS), ROWS)

    def hidden_piece(pair):
        size = len(pair) * GROUP

        def gated(gate, up):
            return (gate / (1.0 + jnp.exp(-gate)) * up).astype(jnp.bfloat16)

        value = gated(acc[:size, 0:256], acc[:size, 256:512])
        last_units = gated(acc[:size, 512:544], acc[:size, 544:576])
        for i, dz in enumerate(pair):
            hid[x, group(dz), :] = value[i * GROUP:(i + 1) * GROUP]
            rows = last_units[i * GROUP:(i + 1) * GROUP]
            tail[x, quarter(dz), :] = jnp.concatenate(
                [rows[n * ROWS:(n + 1) * ROWS] for n in range(4)], axis=1
            )
            h_send(dz, 0)
            h_send(dz, 1)

    def hidden_wait(pair):
        for dz in pair:
            for k in (1, 3, 2):
                at = ((dz % NZ) * 3 + k - 1)
                recv(hid.at[(x + NX - k) % NX, group(dz), :], SEM["h"] + at)
                recv(tail.at[(x + NX - k) % NX, quarter(dz), :], SEM["ht"] + at)
        for i, dz in enumerate(pair):
            packed = [tail[xs, quarter(dz), :] for xs in range(NX)]
            rest[i * GROUP:(i + 1) * GROUP, :] = jnp.concatenate(
                [
                    jnp.concatenate([p[:, n * 32:(n + 1) * 32] for p in packed], axis=1)
                    for n in range(4)
                ],
                axis=0,
            )

    def down_piece(pair, n):
        cols = pl.ds(n * 256, 256)
        size = len(pair) * GROUP
        lower = jnp.concatenate([wd[xs * FF + 256:(xs + 1) * FF, cols] for xs in range(NX)], axis=0)
        total = jnp.dot(rest[:size, :], lower, preferred_element_type=jnp.float32)
        for xs in range(NX):
            rows = jnp.concatenate([hid[xs, group(dz), :] for dz in pair], axis=0)
            total += jnp.dot(
                rows, wd[xs * FF:xs * FF + 256, cols], preferred_element_type=jnp.float32
            )
        for i, dz in enumerate(pair):
            part[group(dz), cols] = total[i * GROUP:(i + 1) * GROUP]

    def queue_up(pair):
        for k in range(D // KCH):
            pieces.append(functools.partial(up_piece, pair, k))
        pieces.append(functools.partial(hidden_piece, pair))

    def queue_down(pair):
        pieces.append(functools.partial(hidden_wait, pair))
        for n in range(SLICE // 256):
            pieces.append(functools.partial(down_piece, pair, n))

    half_cols = (pl.ds(0, HALF), pl.ds(HALF, HALF))

    def ring_step(step):
        for sub in range(SUBS):
            k = sub
            to = (x + k) % NX
            rows = pl.ds(pl.multiple_of(to * ROWS, ROWS), ROWS)
            for way in range(2):
                index = SEM["r"] + (way * 7 + step) * SUBS + sub
                dz = (-1 if way == 0 else 1) * (1 + step)
                value = part[block(k, dz), half_cols[way]]
                if step > 0:
                    recv(rbuf.at[way, step - 1, rows], index - SUBS)
                    value = value + rbuf[way, step - 1, rows].astype(jnp.float32)
                sbuf[way, step, rows] = value.astype(jnp.bfloat16)
                if step < 6:
                    send(sbuf.at[way, step, rows], rbuf.at[way, step, rows], index, toward[way])
                else:
                    send(sbuf.at[way, step, rows], fin.at[way, x], SEM["f"] + way * 4 + k, beside(way, k))

    def near_send():
        for k in range(4):
            value = part[block(k, 0), :].astype(jnp.bfloat16)
            if k == 0:
                near[x] = value
            else:
                own[k] = value
                send(own.at[k], near.at[x], SEM["n"] + k - 1, at_x(k))

    ways = ((0, -1), (1, 1))

    def b1(hop):
        for way, sign in ways:
            b1_recv(way, hop)
            if hop < 4:
                b1_send(way, hop + 1)
                b2_send(sign * hop)
        if hop == 4:
            b2_send(4)

    def a2(hop, j):
        for way, sign in ways:
            a2_recv(way, hop, j)
            if hop < 4:
                a2_send(way, hop + 1, j)

    def last(hop):
        for way, sign in ways[:1 if hop in (0, 4) else 2]:
            b2_last(sign * hop)

    def a1(k):
        recv(xb.at[block(-k, 0), full_a], SEM["a1"] + k - 1)
        for way in range(2):
            a2_send(way, 1, k)

    for k in (1, 3, 2):
        ref = xb.at[mine, full_a]
        send(ref, ref, SEM["a1"] + k - 1, at_x(k))
    for way, sign in ways:
        b1_send(way, 1)
        a2_send(way, 1, 0)
    b2_send(0)
    loads[1].wait()
    loads[2].wait()
    attend(0)
    a1(1)
    a1(3)
    b1(1)
    a1(2)
    for k in (1, 3, 2):
        w1_send(k)
    for load in loads[3:]:
        load.wait()
    for k in range(D // 512):
        pieces.append(functools.partial(turn_piece, k))
    a2(1, 0)
    tick(2)
    b2_pass(0)
    attend(1)
    a2(1, 1)
    tick(3)
    a2(1, 3)
    tick(3)
    b2_pass(-1)
    a2(1, 2)
    tick(3)
    b2_pass(1)
    drain()
    b1(2)
    a2(2, 0)
    tick(4)
    attend(2)
    last(0)
    a2(2, 1)
    drain()
    last(1)
    queue_up((-1, 0, 1))
    tick(2)
    w1_pass(1)
    a2(2, 3)
    tick(2)
    b2_pass(-2)
    w1_pass(3)
    a2(2, 2)
    tick(2)
    b2_pass(2)
    w1_pass(2)
    b1(3)
    drain()
    a2(3, 0)
    attend(3)
    a2(3, 1)
    last(2)
    queue_up((-2, 2))
    tick(2)
    for m in (1, 3, 2):
        w2_pass(1, m)
    a2(3, 3)
    tick(2)
    b2_pass(-3)
    for m in (1, 3, 2):
        w2_pass(3, m)
    a2(3, 2)
    tick(2)
    b2_pass(3)
    for m in (1, 3, 2):
        w2_pass(2, m)
    drain()
    b1(4)
    for k in (1, 2, 3):
        for m in range(4):
            wc_recv(k, m)
    queue_down((-1, 0, 1))
    drain()
    ring_step(0)
    a2(4, 0)
    last(3)
    queue_up((-3, 3))
    drain()
    a2(4, 1)
    queue_down((-2, 2))
    drain()
    ring_step(1)
    a2(4, 3)
    a2(4, 2)
    for k in range(CA // KCH):
        up_piece((4,), k)
    b2_far()
    for k in range(CA // KCH, D // KCH):
        up_piece((4,), k)
    hidden_piece((4,))
    near_send()
    queue_down((-3, 3))
    drain()
    ring_step(2)
    queue_down((4,))
    drain()
    for step in range(3, 6):
        ring_step(step)
    ring_step(6)
    for copy in sent:
        copy.wait_send()
    for k in (1, 2, 3):
        recv(near.at[(x + NX - k) % NX], SEM["n"] + k - 1)
    for way in range(2):
        for k in range(4):
            recv(fin.at[way, (x + NX - k) % NX], SEM["f"] + way * 4 + k)
    for xs in range(NX):
        for way in range(2):
            value = near[xs, :, half_cols[way]].astype(jnp.float32) + fin[way, xs].astype(jnp.float32)
            ffn_out[:, xs * SLICE + way * HALF:xs * SLICE + (way + 1) * HALF] = value.astype(jnp.bfloat16)


def body(rows, counts, gate, up, down, queries, cache, live, lengths):
    bf16, f32 = jnp.bfloat16, jnp.float32
    smem = pl.BlockSpec(memory_space=pltpu.SMEM)
    hbm = pl.BlockSpec(memory_space=pl.ANY)
    vmem = pl.BlockSpec(memory_space=pltpu.VMEM)
    return pl.pallas_call(
        kernel,
        out_shape=(
            jax.ShapeDtypeStruct((ROWS, D), bf16),
            jax.ShapeDtypeStruct((4, 64, LATENT), bf16),
        ),
        in_specs=[smem] * 3 + [hbm] * 6,
        out_specs=(vmem, vmem),
        scratch_shapes=[
            pltpu.VMEM((ROWS, D), bf16),
            pltpu.VMEM((NZ * GROUP, D), bf16),
            pltpu.VMEM((2 * FF, D), bf16),
            pltpu.VMEM((D, 2 * FF), bf16),
            pltpu.VMEM((NX * FF, SLICE), bf16),
            pltpu.VMEM((4, 64, 576), bf16),
            pltpu.VMEM((4, 64, 576), bf16),
            pltpu.VMEM((3 * GROUP, 2 * FF), f32),
            pltpu.VMEM((NX, NZ * GROUP, 256), bf16),
            pltpu.VMEM((NX, NZ * ROWS, 128), bf16),
            pltpu.VMEM((3 * GROUP, 128), bf16),
            pltpu.VMEM((NZ * GROUP, SLICE), f32),
            pltpu.VMEM((2, 7, GROUP, HALF), bf16),
            pltpu.VMEM((2, 6, GROUP, HALF), bf16),
            pltpu.VMEM((NX, ROWS, SLICE), bf16),
            pltpu.VMEM((NX, ROWS, SLICE), bf16),
            pltpu.VMEM((2, NX, ROWS, HALF), bf16),
            pltpu.SemaphoreType.DMA((NSEM,)),
            pltpu.SemaphoreType.DMA((NSEM,)),
            pltpu.SemaphoreType.DMA((8,)),
        ],
        compiler_params=pltpu.CompilerParams(
            collective_id=1, has_side_effects=True, vmem_limit_bytes=56 * 2**20
        ),
        cost_estimate=pl.CostEstimate(
            flops=2 * 512 * D * FF * 3, bytes_accessed=16 * 2**20, transcendentals=512 * FF
        ),
    )(counts, live, lengths, rows, gate.T, up.T, down, queries, cache)


def solution(mesh):
    placed = (
        P(("inst", "rank"), None),
        P("inst"),
        P(None, "rank"),
        P(None, "rank"),
        P("rank", None),
        P(("inst", "rank"), None, None),
        P(("inst", "rank"), None, None),
        P("inst"),
        P("inst"),
    )
    return jax.shard_map(
        body,
        mesh=mesh,
        in_specs=placed,
        out_specs=(P(("inst", "rank"), None), P(("inst", "rank"), None, None)),
        check_vma=False,
    )
```

```python
import functools

import jax
import jax.numpy as jnp
from jax import lax
from jax.experimental import pallas as pl
from jax.experimental.pallas import tpu as pltpu
from jax.sharding import PartitionSpec as P

MESH = pl.DeviceIdType.MESH
D, FF, ROWS, LATENT = 7168, 288, 16, 512
NX, NZ, NY = 4, 8, 4
GROUP = NX * ROWS
SLICE = D // NX
HALF = SLICE // 2
TILE = 128
CA = 30 * TILE
A0 = 15 * TILE
CB = D - CA
B0 = 13 * TILE
KCH = 1792
SUBS, SUB = 4, 16
score_scale = 192.0 ** (-0.5)


def layout():
    names = {}

    def add(name, count):
        names[name] = len_box[0]
        len_box[0] += count

    len_box = [0]
    add("a1", 3)
    add("b1", 8)
    add("a2", 32)
    add("b2", 32)
    add("w1", 3)
    add("w2", 9)
    add("wc", 12)
    add("h", 24)
    add("ht", 24)
    add("r", 56)
    add("f", 8)
    add("n", 3)
    return names, len_box[0]


SEM, NSEM = layout()


def kernel(
    counts, live, lengths, rows_in, wg_in, wu_in, wd_in, q_in, c_in, ffn_out, attn_out,
    xi, xb, wgu, wgt, wd, qb, cb, acc, hid, tail, rest, part, sbuf, rbuf, near, own, fin, ssem, rsem, lsem,
):
    inst = lax.axis_index("inst")
    rank = lax.axis_index("rank")
    y, c = inst // 2, inst % 2
    x, z = rank // NZ, rank % NZ
    yhi, ylo = y // 2, y % 2

    def at_x(k):
        return (inst, ((x + NX + k) % NX) * NZ + z)

    def at_z(k):
        return (inst, x * NZ + (z + NZ + k) % NZ)

    def at_y(k):
        return (((y + NY + k) % NY) * 2 + c, rank)

    other = (y * 2 + (1 - c), rank)
    zp, zm, xp, xm = at_z(1), at_z(-1), at_x(1), at_x(-1)

    def beside(way, k):
        return (inst, ((x + k) % NX) * NZ + (z + NZ + (1 if way == 0 else -1)) % NZ)


    loads = [
        pltpu.make_async_copy(rows_in, xi, lsem.at[0]),
        pltpu.make_async_copy(q_in, qb, lsem.at[1]),
        pltpu.make_async_copy(c_in, cb, lsem.at[2]),
        pltpu.make_async_copy(wg_in.at[0:256, :], wgu.at[0:256, :], lsem.at[3]),
        pltpu.make_async_copy(wu_in.at[0:256, :], wgu.at[256:512, :], lsem.at[4]),
        pltpu.make_async_copy(wg_in.at[256:288, :], wgu.at[512:544, :], lsem.at[6]),
        pltpu.make_async_copy(wu_in.at[256:288, :], wgu.at[544:576, :], lsem.at[7]),
        pltpu.make_async_copy(
            wd_in.at[:, pl.ds(pl.multiple_of(x * SLICE, TILE), SLICE)],
            wd.at[pl.ds(pl.multiple_of(x * FF, 16), FF), :],
            lsem.at[5],
        ),
    ]
    loads[0].start()

    barrier = pltpu.get_barrier_semaphore()
    peers = [zp, zm, xp, xm, at_x(2), at_y(1), at_y(-1), at_y(2), other]
    peers += [beside(way, k) for way in range(2) for k in (1, 2, 3)]
    for peer in peers:
        pl.semaphore_signal(barrier, inc=1, device_id=peer, device_id_type=MESH)
    for load in loads[1:]:
        load.start()
    loads[0].wait()
    mine = pl.ds(pl.multiple_of((z * NX + x) * ROWS, ROWS), ROWS)
    row_live = lax.broadcasted_iota(jnp.int32, (ROWS, 1), 0) < counts[rank]
    xb[mine, :] = jnp.where(row_live, xi[...], jnp.zeros_like(xi[...]))
    pl.semaphore_wait(barrier, len(peers))

    sent = []

    def send(src, dst, index, peer):
        copy = pltpu.make_async_remote_copy(
            src, dst, ssem.at[index], rsem.at[index], device_id=peer, device_id_type=MESH
        )
        copy.start()
        sent.append(copy)

    def settle(count):
        for _ in range(count):
            sent.pop(0).wait_send()

    def recv(dst, index):
        pltpu.make_async_remote_copy(
            dst, dst, ssem.at[index], rsem.at[index], device_id=zp, device_id_type=MESH
        ).wait_recv()

    def block(dx, dz):
        at = ((z + NZ + dz) % NZ) * NX + (x + NX + dx) % NX
        return pl.ds(pl.multiple_of(at * ROWS, ROWS), ROWS)

    def group(dz):
        return pl.ds(pl.multiple_of(((z + NZ + dz) % NZ) * GROUP, GROUP), GROUP)

    full_a, half_a = pl.ds(0, CA), (pl.ds(0, A0), pl.ds(A0, CA - A0))
    full_b, half_b = pl.ds(CA, CB), (pl.ds(CA, B0), pl.ds(CA + B0, CB - B0))
    toward = (zp, zm)

    def a2_index(way, hop, j):
        return SEM["a2"] + (way * 4 + hop - 1) * 4 + j

    def b1_index(way, hop):
        return SEM["b1"] + way * 4 + hop - 1

    def a2_send(way, hop, j):
        sign = -1 if way == 0 else 1
        cols = full_a if hop < 4 else half_a[way]
        ref = xb.at[block(-j, sign * (hop - 1)), cols]
        send(ref, ref, a2_index(way, hop, j), toward[way])

    def a2_recv(way, hop, j):
        sign = -1 if way == 0 else 1
        cols = full_a if hop < 4 else half_a[way]
        recv(xb.at[block(-j, sign * hop), cols], a2_index(way, hop, j))

    def b1_send(way, hop):
        sign = -1 if way == 0 else 1
        cols = full_b if hop < 4 else half_b[way]
        ref = xb.at[block(0, sign * (hop - 1)), cols]
        send(ref, ref, b1_index(way, hop), toward[way])

    def b1_recv(way, hop):
        sign = -1 if way == 0 else 1
        cols = full_b if hop < 4 else half_b[way]
        recv(xb.at[block(0, sign * hop), cols], b1_index(way, hop))

    def b2_index(dz, kind):
        return SEM["b2"] + (dz % NZ) * 4 + kind

    def b2_send(dz):
        ref = xb.at[block(0, dz), full_b]
        send(ref, ref, b2_index(dz, 0), xp)
        send(ref, ref, b2_index(dz, 1), xm)
        if dz == 4:
            send(ref, ref, b2_index(dz, 2), at_x(2))

    def b2_pass(dz):
        recv(xb.at[block(-1, dz), full_b], b2_index(dz, 0))
        ref = xb.at[block(-1, dz), half_b[0]]
        send(ref, ref, b2_index(dz, 2), xp)
        recv(xb.at[block(1, dz), full_b], b2_index(dz, 1))
        ref = xb.at[block(1, dz), half_b[1]]
        send(ref, ref, b2_index(dz, 3), xm)

    def b2_far():
        for k, kind in ((1, 0), (3, 1), (2, 2)):
            recv(xb.at[block(-k, 4), full_b], b2_index(4, kind))

    def b2_last(dz):
        recv(xb.at[block(-2, dz), half_b[0]], b2_index(dz, 2))
        recv(xb.at[block(2, dz), half_b[1]], b2_index(dz, 3))

    def wd_piece(xs, yy, start, count):
        row = xs * FF + (yy // 2) * 144 + start
        col = (yy % 2) * HALF
        return wd.at[pl.ds(pl.multiple_of(row, 16), count), pl.ds(pl.multiple_of(col, TILE), HALF)]

    def w1_send(k):
        to = (x + k) % NX
        src = wd_in.at[
            pl.ds(pl.multiple_of(yhi * 144 + c * 64, 16), 80),
            pl.ds(pl.multiple_of(to * SLICE + ylo * HALF, TILE), HALF),
        ]
        send(src, wd_piece(x, y, c * 64, 80), SEM["w1"] + k - 1, at_x(k))

    def wc_send(k, m):
        ref = wd_piece((x + NX - k) % NX, (y + NY - m) % NY, c * 80, 64)
        send(ref, ref, SEM["wc"] + (k - 1) * 4 + m, other)

    def w1_pass(k):
        ref = wd_piece((x + NX - k) % NX, y, c * 64, 80)
        recv(ref, SEM["w1"] + k - 1)
        for m in (1, 3, 2):
            send(ref, ref, SEM["w2"] + (k - 1) * 3 + m - 1, at_y(m))
        wc_send(k, 0)

    def w2_pass(k, m):
        ref = wd_piece((x + NX - k) % NX, (y + NY - m) % NY, c * 64, 80)
        recv(ref, SEM["w2"] + (k - 1) * 3 + m - 1)
        wc_send(k, m)

    def wc_recv(k, m):
        ref = wd_piece((x + NX - k) % NX, (y + NY - m) % NY, (1 - c) * 80, 64)
        recv(ref, SEM["wc"] + (k - 1) * 4 + m)

    pieces = []

    def tick(count=1):
        for _ in range(count):
            if pieces:
                pieces.pop(0)()

    def drain():
        while pieces:
            pieces.pop(0)()

    def attend(slot):
        keys = cb[slot]
        scores = lax.dot_general(
            qb[slot], keys, (((1,), (1,)), ((), ())), preferred_element_type=jnp.float32
        ) * score_scale
        places = lax.broadcasted_iota(jnp.int32, scores.shape, 1)
        scores = jnp.where(places < lengths[rank * 4 + slot], scores, -1e30)
        expo = jnp.exp(scores - jnp.max(scores, axis=1, keepdims=True))
        probs = (expo / jnp.sum(expo, axis=1, keepdims=True)).astype(jnp.bfloat16)
        value = jnp.dot(probs, keys[:, :LATENT], preferred_element_type=jnp.float32)
        keep = jnp.full((1, 1), slot, jnp.int32) < live[rank]
        attn_out[slot] = jnp.where(keep, value, 0.0).astype(jnp.bfloat16)

    def turn_piece(k):
        cols = pl.ds(k * 512, 512)
        wgt[cols, :] = wgu[:, cols].T

    def up_piece(pair, k):
        cols = pl.ds(k * KCH, KCH)
        rows = jnp.concatenate([xb[group(dz), cols] for dz in pair], axis=0)
        term = jnp.dot(rows, wgt[cols, :], preferred_element_type=jnp.float32)
        size = len(pair) * GROUP
        if k == 0:
            acc[:size] = term
        else:
            acc[:size] += term

    def h_send(dz, part_of):
        for k in (2, 1, 3):
            at = ((dz % NZ) * 3 + k - 1)
            if part_of == 0:
                ref = hid.at[x, group(dz), :]
                send(ref, ref, SEM["h"] + at, at_x(k))
            else:
                ref = tail.at[x, quarter(dz), :]
                send(ref, ref, SEM["ht"] + at, at_x(k))

    def quarter(dz):
        return pl.ds(pl.multiple_of(((z + NZ + dz) % NZ) * ROWS, ROWS), ROWS)

    def hidden_piece(pair):
        size = len(pair) * GROUP

        def gated(gate, up):
            return (gate / (1.0 + jnp.exp(-gate)) * up).astype(jnp.bfloat16)

        value = gated(acc[:size, 0:256], acc[:size, 256:512])
        last_units = gated(acc[:size, 512:544], acc[:size, 544:576])
        for i, dz in enumerate(pair):
            hid[x, group(dz), :] = value[i * GROUP:(i + 1) * GROUP]
            rows = last_units[i * GROUP:(i + 1) * GROUP]
            tail[x, quarter(dz), :] = jnp.concatenate(
                [rows[n * ROWS:(n + 1) * ROWS] for n in range(4)], axis=1
            )
            h_send(dz, 0)
            h_send(dz, 1)

    def hidden_wait(pair):
        for dz in pair:
            for k in (1, 3, 2):
                at = ((dz % NZ) * 3 + k - 1)
                recv(hid.at[(x + NX - k) % NX, group(dz), :], SEM["h"] + at)
                recv(tail.at[(x + NX - k) % NX, quarter(dz), :], SEM["ht"] + at)
        for i, dz in enumerate(pair):
            packed = [tail[xs, quarter(dz), :] for xs in range(NX)]
            rest[i * GROUP:(i + 1) * GROUP, :] = jnp.concatenate(
                [
                    jnp.concatenate([p[:, n * 32:(n + 1) * 32] for p in packed], axis=1)
                    for n in range(4)
                ],
                axis=0,
            )

    def down_piece(pair, n):
        cols = pl.ds(n * 256, 256)
        size = len(pair) * GROUP
        lower = jnp.concatenate([wd[xs * FF + 256:(xs + 1) * FF, cols] for xs in range(NX)], axis=0)
        total = jnp.dot(rest[:size, :], lower, preferred_element_type=jnp.float32)
        for xs in range(NX):
            rows = jnp.concatenate([hid[xs, group(dz), :] for dz in pair], axis=0)
            total += jnp.dot(
                rows, wd[xs * FF:xs * FF + 256, cols], preferred_element_type=jnp.float32
            )
        for i, dz in enumerate(pair):
            part[group(dz), cols] = total[i * GROUP:(i + 1) * GROUP]

    def queue_up(pair):
        for k in range(D // KCH):
            pieces.append(functools.partial(up_piece, pair, k))
        pieces.append(functools.partial(hidden_piece, pair))

    def queue_down(pair):
        pieces.append(functools.partial(hidden_wait, pair))
        for n in range(SLICE // 256):
            pieces.append(functools.partial(down_piece, pair, n))

    half_cols = (pl.ds(0, HALF), pl.ds(HALF, HALF))

    def ring_step(step):
        for sub in (2, 1, 3, 0):
            k = sub
            to = (x + k) % NX
            rows = pl.ds(pl.multiple_of(to * ROWS, ROWS), ROWS)
            for way in range(2):
                index = SEM["r"] + (way * 7 + step) * SUBS + sub
                dz = (-1 if way == 0 else 1) * (1 + step)
                value = part[block(k, dz), half_cols[way]]
                if step > 0:
                    recv(rbuf.at[way, step - 1, rows], index - SUBS)
                    value = value + rbuf[way, step - 1, rows].astype(jnp.float32)
                sbuf[way, step, rows] = value.astype(jnp.bfloat16)
                if step < 6:
                    send(sbuf.at[way, step, rows], rbuf.at[way, step, rows], index, toward[way])
                else:
                    send(sbuf.at[way, step, rows], fin.at[way, x], SEM["f"] + way * 4 + k, beside(way, k))

    def near_send():
        for k in range(4):
            value = part[block(k, 0), :].astype(jnp.bfloat16)
            if k == 0:
                near[x] = value
            else:
                own[k] = value
                send(own.at[k], near.at[x], SEM["n"] + k - 1, at_x(k))

    ways = ((0, -1), (1, 1))

    def b1(hop):
        for way, sign in ways:
            b1_recv(way, hop)
            if hop < 4:
                b1_send(way, hop + 1)
                b2_send(sign * hop)
        if hop == 4:
            b2_send(4)

    def a2(hop, j):
        for way, sign in ways:
            a2_recv(way, hop, j)
            if hop < 4:
                a2_send(way, hop + 1, j)

    def last(hop):
        for way, sign in ways[:1 if hop in (0, 4) else 2]:
            b2_last(sign * hop)

    def a1(k):
        recv(xb.at[block(-k, 0), full_a], SEM["a1"] + k - 1)
        for way in range(2):
            a2_send(way, 1, k)

    for k in (1, 3, 2):
        ref = xb.at[mine, full_a]
        send(ref, ref, SEM["a1"] + k - 1, at_x(k))
    for way, sign in ways:
        b1_send(way, 1)
        a2_send(way, 1, 0)
    b2_send(0)
    loads[1].wait()
    loads[2].wait()
    attend(0)
    attend(1)
    for k in (1, 3, 2):
        w1_send(k)
    b1(1)
    a1(1)
    a1(3)
    tick(3)
    b1(2)
    for load in loads[3:]:
        load.wait()
    for k in range(D // 512):
        pieces.append(functools.partial(turn_piece, k))
    a1(2)
    w1_pass(3)
    b2_pass(0)
    a2(1, 1)
    drain()
    a2(1, 0)
    a2(1, 2)
    tick(3)
    tick(2)
    attend(3)
    b2_pass(-1)
    b2_pass(1)
    b1(3)
    tick(2)
    a2(1, 3)
    tick(2)
    last(0)
    b2_pass(2)
    a2(2, 0)
    a2(2, 1)
    tick(3)
    attend(2)
    w1_pass(1)
    a2(2, 2)
    tick(2)
    b2_pass(-2)
    last(1)
    queue_up((-1, 0, 1))
    drain()
    b2_pass(-3)
    a2(2, 3)
    b2_pass(3)
    w1_pass(2)
    last(2)
    for m in (1, 3, 2):
        w2_pass(1, m)
    queue_up((-2, 2))
    tick(2)
    tick(2)
    tick(2)
    a2(3, 1)
    for m in (1, 3, 2):
        w2_pass(3, m)
    b1(4)
    a2(3, 3)
    for m in (1, 3, 2):
        w2_pass(2, m)
    a2(3, 0)
    for k in (1, 2, 3):
        for m in range(4):
            wc_recv(k, m)
    queue_down((-1, 0, 1))
    drain()
    last(3)
    a2(3, 2)
    ring_step(0)
    queue_up((-3, 3))
    queue_down((-2, 2))
    drain()
    ring_step(1)
    a2(4, 2)
    a2(4, 1)
    a2(4, 0)
    b2_far()
    a2(4, 3)
    for k in range(CA // KCH):
        up_piece((4,), k)
    drain()
    queue_down((-3, 3))
    for k in range(CA // KCH, D // KCH):
        up_piece((4,), k)
    hidden_piece((4,))
    drain()
    ring_step(2)
    near_send()
    drain()
    queue_down((4,))
    drain()
    for step in range(3, 7):
        before = len(sent)
        ring_step(step)
        settle(before)
    for k in (1, 2, 3):
        recv(near.at[(x + NX - k) % NX], SEM["n"] + k - 1)
    for way in range(2):
        for k in range(4):
            recv(fin.at[way, (x + NX - k) % NX], SEM["f"] + way * 4 + k)
    settle(len(sent))
    for xs in range(NX):
        for way in range(2):
            value = near[xs, :, half_cols[way]].astype(jnp.float32) + fin[way, xs].astype(jnp.float32)
            ffn_out[:, xs * SLICE + way * HALF:xs * SLICE + (way + 1) * HALF] = value.astype(jnp.bfloat16)


def body(rows, counts, gate, up, down, queries, cache, live, lengths):
    bf16, f32 = jnp.bfloat16, jnp.float32
    smem = pl.BlockSpec(memory_space=pltpu.SMEM)
    hbm = pl.BlockSpec(memory_space=pl.ANY)
    vmem = pl.BlockSpec(memory_space=pltpu.VMEM)
    return pl.pallas_call(
        kernel,
        out_shape=(
            jax.ShapeDtypeStruct((ROWS, D), bf16),
            jax.ShapeDtypeStruct((4, 64, LATENT), bf16),
        ),
        in_specs=[smem] * 3 + [hbm] * 6,
        out_specs=(vmem, vmem),
        scratch_shapes=[
            pltpu.VMEM((ROWS, D), bf16),
            pltpu.VMEM((NZ * GROUP, D), bf16),
            pltpu.VMEM((2 * FF, D), bf16),
            pltpu.VMEM((D, 2 * FF), bf16),
            pltpu.VMEM((NX * FF, SLICE), bf16),
            pltpu.VMEM((4, 64, 576), bf16),
            pltpu.VMEM((4, 64, 576), bf16),
            pltpu.VMEM((3 * GROUP, 2 * FF), f32),
            pltpu.VMEM((NX, NZ * GROUP, 256), bf16),
            pltpu.VMEM((NX, NZ * ROWS, 128), bf16),
            pltpu.VMEM((3 * GROUP, 128), bf16),
            pltpu.VMEM((NZ * GROUP, SLICE), f32),
            pltpu.VMEM((2, 7, GROUP, HALF), bf16),
            pltpu.VMEM((2, 6, GROUP, HALF), bf16),
            pltpu.VMEM((NX, ROWS, SLICE), bf16),
            pltpu.VMEM((NX, ROWS, SLICE), bf16),
            pltpu.VMEM((2, NX, ROWS, HALF), bf16),
            pltpu.SemaphoreType.DMA((NSEM,)),
            pltpu.SemaphoreType.DMA((NSEM,)),
            pltpu.SemaphoreType.DMA((8,)),
        ],
        compiler_params=pltpu.CompilerParams(
            collective_id=1, has_side_effects=True, vmem_limit_bytes=56 * 2**20
        ),
        cost_estimate=pl.CostEstimate(
            flops=2 * 512 * D * FF * 3, bytes_accessed=16 * 2**20, transcendentals=512 * FF
        ),
    )(counts, live, lengths, rows, gate.T, up.T, down, queries, cache)


def solution(mesh):
    placed = (
        P(("inst", "rank"), None),
        P("inst"),
        P(None, "rank"),
        P(None, "rank"),
        P("rank", None),
        P(("inst", "rank"), None, None),
        P(("inst", "rank"), None, None),
        P("inst"),
        P("inst"),
    )
    return jax.shard_map(
        body,
        mesh=mesh,
        in_specs=placed,
        out_specs=(P(("inst", "rank"), None), P(("inst", "rank"), None, None)),
        check_vma=False,
    )
```
